1024 devices in a mesh: dp: 16 (over y, x_hi, core), shard: 64 (over x_lo, z).
Axes of the slice: x: 4 (x_hi: 2, x_lo: 2; x = x_hi * 2 + x_lo), y: 4, z: 32, core: 2. Of those that a mesh axis runs over, the one named last changes fastest.
Arguments:
- feats: bfloat16 [524288, 3072], P(('dp', 'shard')), may hold values from -24 to 24
- w_qkv: bfloat16 [3072, 384], P('shard'), may hold values from -0.125 to 0.125
- grad_out: bfloat16 [524288, 128], P(('dp', 'shard')), may hold values from -6 to 6
- block_mask: int32 [1024, 4, 4], P(('dp', 'shard')), may hold values from 0 to 1, as said below
- counts: int32 [1024], P(('dp', 'shard')), may hold values from 128 to 512
Outputs:
- attended: bfloat16 [524288, 128], P(('dp', 'shard'))
- grad_w: float32 [3072, 384], P('shard')
The draws below stay inside these ranges and needn't reach their ends.
Inputs may be any that keep to these rules, and one draw needn't show every extreme that they name: block_mask[c, b, 0] and block_mask[c, b, b] are 1 for every block b.
All inputs are finite; a program needn't handle non-finite values.
Results may differ from the reference program's by a relative error of at most 0.029.
Values may be sent and summed in bfloat16 or wider, within the bound.
No kernel may reach another device: no remote copies, remote signals or barrier semaphores. Data moves between devices by JAX's collectives and lax.ppermute only.
A program may use at most 32 MiB of HBM per device.

```python
import math
import jax
import jax.numpy as jnp
from jax import lax

D_WIN = 3072
HD = 128
BLK = 128
LEN = 512
NB = 4
COMPLEXES = 1024
TOKENS = 524288


aligned_rows = 128


def shared_rows(key):
    order = jax.random.permutation(jax.random.fold_in(key, 101), D_WIN)
    return order < aligned_rows


def draw_w_qkv(key, part):
    shared = shared_rows(key)
    key = jax.random.fold_in(key, 5)
    first_key, second_key, third_key = jax.random.split(key, 3)
    shape = (D_WIN, HD)
    base_query = jax.random.truncated_normal(first_key, -4.0, 4.0, shape, jnp.float32)
    base_key = jax.random.truncated_normal(second_key, -4.0, 4.0, shape, jnp.float32)
    base_value = jax.random.truncated_normal(third_key, -4.0, 4.0, shape, jnp.float32)
    scale = 1.0 / math.sqrt(D_WIN)
    w_query = base_query * scale
    w_key = jnp.where(shared[:, None], w_query, base_key * scale)
    w_value = base_value * scale
    return jnp.concatenate([w_query, w_key, w_value], axis=1).astype(jnp.bfloat16)


def draw_feats(key, part):
    shared = shared_rows(key)
    key = jax.random.fold_in(key, 7)
    pair_key, pick_key, level_key, row_key = jax.random.split(key, 4)
    paired = jax.random.permutation(pair_key, COMPLEXES).astype(jnp.int32)
    chosen = jax.random.randint(pick_key, (COMPLEXES,), 0, 8) == 0
    chosen = chosen.at[0].set(True)
    levels = jnp.array([14.0, 16.0, 18.0], jnp.float32)
    level = levels[jax.random.randint(level_key, (COMPLEXES,), 0, 3)]
    width_block = D_WIN // COMPLEXES
    column_block = jnp.arange(D_WIN, dtype=jnp.int32) // width_block
    kappa = aligned_rows * math.sqrt(HD) / D_WIN
    spread = math.sqrt(aligned_rows / D_WIN)

    def one(index):
        local = jax.random.fold_in(row_key, index)
        draw_key = jax.random.fold_in(local, 0)
        sign_key = jax.random.fold_in(local, 2)
        rows = jax.random.truncated_normal(draw_key, -4.5, 4.5, (LEN, D_WIN), jnp.float32)
        factor = jnp.where(column_block == paired[index], jnp.float32(5.0), jnp.float32(1.0))
        rows = rows * factor[None, :]
        signs = (jax.random.randint(sign_key, (D_WIN,), 0, 2) * 2 - 1).astype(jnp.float32)
        strength = level[index]
        gap = 2.0 / (kappa * strength)
        mixing = 1.2 / (strength * spread)
        lead = jnp.where(shared, strength * signs, rows[1])
        follow = jnp.where(shared, (strength - gap) * signs, rows[1] + mixing * rows[2])
        rows = rows.at[1].set(jnp.where(chosen[index], lead, rows[1]))
        rows = rows.at[2].set(jnp.where(chosen[index], follow, rows[2]))
        return jnp.clip(rows, -24.0, 24.0).astype(jnp.bfloat16)
    shaped = lax.map(one, jnp.arange(COMPLEXES, dtype=jnp.int32))
    return shaped.reshape(TOKENS, D_WIN)


def draw_block_mask(key, part):
    key = jax.random.fold_in(key, 11)
    bits = jax.random.randint(key, (COMPLEXES, NB, NB), 0, 2)
    column = jnp.arange(NB, dtype=jnp.int32)
    fixed = (column[None, :] == 0) | (column[None, :] == column[:, None])
    return jnp.where(fixed[None, :, :], 1, bits).astype(jnp.int32)


def draw_counts(key, part):
    key = jax.random.fold_in(key, 23)
    values = jax.random.randint(key, (COMPLEXES,), BLK, LEN + 1)
    return values.at[0].set(LEN).astype(jnp.int32)


def block_scale(stream_key, extent, shards, smallest, top_value):
    factor_of = 1.0
    for dim, parts in shards:
        draws = jax.random.uniform(jax.random.fold_in(jax.random.fold_in(stream_key, 6), dim), (parts,), jnp.float32, smallest / len(shards), top_value / len(shards))
        factor_of = factor_of * jnp.repeat(jnp.exp(draws), extent[dim] // parts).reshape((-1,) + (1,) * (len(extent) - 1 - dim))
    return factor_of


def centred(rng, extent, width, most, cuts=(), kind=jnp.bfloat16):
    values = jax.random.normal(rng, extent, jnp.float32) * width
    if len(cuts) > 0:
        values = block_scale(rng, extent, cuts, -0.22, 0.18) * values
    return jnp.clip(values, min=-most, max=most).astype(kind)


def setup_inputs(seed: int = 0) -> dict:
    key_of = jax.random.split(jax.random.key(seed), 6)
    feats = draw_feats(jax.random.fold_in(key_of[5], 71), 0)
    w_qkv = draw_w_qkv(jax.random.fold_in(key_of[5], 71), 0)
    grad_out = centred(key_of[2], (TOKENS, HD), 1.0, 6.0, ((0, 1024),))
    block_mask = draw_block_mask(jax.random.fold_in(key_of[5], 71), 0)
    counts = draw_counts(jax.random.fold_in(key_of[5], 71), 0)
    return dict(feats=feats, w_qkv=w_qkv, grad_out=grad_out, block_mask=block_mask, counts=counts)


def head_pass(rows, weights, cotangent, mask, count):
    qkv = jnp.dot(rows, weights, preferred_element_type=jnp.float32).astype(jnp.bfloat16)
    query = qkv[:, :HD]
    keys = qkv[:, HD:2 * HD]
    values = qkv[:, 2 * HD:]
    factor = 1.0 / jnp.sqrt(jnp.float32(HD))
    scores = jnp.dot(query, keys.T, preferred_element_type=jnp.float32) * factor
    expanded = jnp.repeat(jnp.repeat(mask, BLK, axis=0), BLK, axis=1)
    position = jnp.arange(LEN, dtype=jnp.int32)
    live = (expanded > 0) & (position[None, :] < count)
    scores = jnp.where(live, scores, jnp.float32(-1e+30))
    top = lax.optimization_barrier(jnp.max(scores, axis=1, keepdims=True))
    weight = jnp.where(live, jnp.exp(scores - top), jnp.float32(0.0))
    probs = weight / lax.optimization_barrier(jnp.sum(weight, axis=1, keepdims=True))
    probs_b = probs.astype(jnp.bfloat16)
    output = jnp.dot(probs_b, values, preferred_element_type=jnp.float32).astype(jnp.bfloat16)
    grad_values = jnp.dot(probs_b.T, cotangent, preferred_element_type=jnp.float32)
    dprobs = jnp.dot(cotangent, values.T, preferred_element_type=jnp.float32)
    delta = lax.optimization_barrier(jnp.sum(cotangent.astype(jnp.float32) * output.astype(jnp.float32), axis=1, keepdims=True))
    dscore = (probs * (dprobs - delta) * factor).astype(jnp.bfloat16)
    grad_query = jnp.dot(dscore, keys, preferred_element_type=jnp.float32)
    grad_keys = jnp.dot(dscore.T, query, preferred_element_type=jnp.float32)
    d_qkv = jnp.concatenate([grad_query, grad_keys, grad_values], axis=1).astype(jnp.bfloat16)
    return (output, d_qkv)

def reference(feats, w_qkv, grad_out, block_mask, counts):
    shaped = feats.reshape(COMPLEXES, LEN, D_WIN)
    cot = grad_out.reshape(COMPLEXES, LEN, HD)

    def one(items):
        return head_pass(items[0], w_qkv, items[1], items[2], items[3])
    outputs, grads = lax.map(one, (shaped, cot, block_mask, counts))
    attended = outputs.reshape(TOKENS, HD)
    flat = grads.reshape(TOKENS, 3 * HD)
    grad_w = lax.dot_general(feats, flat, (((0,), (0,)), ((), ())), preferred_element_type=jnp.float32)
    return (attended, grad_w)
```

```python
import jax
import jax.numpy as jnp
from jax import lax
from jax.sharding import Mesh
from jax.sharding import PartitionSpec as P

BF16 = jnp.bfloat16
F32 = jnp.float32
DP = ("y", "xh", "core")
SHARD = ("xl", "z")
CHIPS = ("xl", "y", "xh")
SWAP = [(0, 1), (1, 0)]


def attention_pass(qkv, cotangent, mask, count, length, block, head):
    query = qkv[:, :head]
    keys = qkv[:, head : 2 * head]
    values = qkv[:, 2 * head :]
    factor = 1.0 / jnp.sqrt(F32(head))
    scores = jnp.dot(query, keys.T, preferred_element_type=F32) * factor
    expanded = jnp.repeat(jnp.repeat(mask, block, axis=0), block, axis=1)
    position = jnp.arange(length, dtype=jnp.int32)
    live = (expanded > 0) & (position[None, :] < count)
    scores = jnp.where(live, scores, F32(-1e30))
    top = jnp.max(scores, axis=1, keepdims=True)
    weight = jnp.where(live, jnp.exp(scores - top), F32(0.0))
    probs = weight / jnp.sum(weight, axis=1, keepdims=True)
    probs_b = probs.astype(BF16)
    output = jnp.dot(probs_b, values, preferred_element_type=F32).astype(BF16)
    grad_values = jnp.dot(probs_b.T, cotangent, preferred_element_type=F32)
    dprobs = jnp.dot(cotangent, values.T, preferred_element_type=F32)
    delta = jnp.sum(cotangent.astype(F32) * output.astype(F32), axis=1, keepdims=True)
    dscore = (probs * (dprobs - delta) * factor).astype(BF16)
    grad_query = jnp.dot(dscore, keys, preferred_element_type=F32)
    grad_keys = jnp.dot(dscore.T, query, preferred_element_type=F32)
    d_qkv = jnp.concatenate([grad_query, grad_keys, grad_values], axis=1).astype(BF16)
    return (output, d_qkv)


def contract_rows(columns, d_qkv):
    return lax.dot_general(columns, d_qkv, (((0,), (0,)), ((), ())), preferred_element_type=F32)


def reordered(feats, core, n_xl, n_z, n_dp, unit):
    depth = feats.shape[1] // n_xl
    half = n_dp // 2
    line = n_z * unit
    at = lax.broadcasted_iota(jnp.int32, (depth, depth // 2), 1)
    pair, z, row = at // line, (at % line) // unit, at % unit
    source = z * (n_dp * unit) + (2 * pair + core) * unit + row
    pick = (lax.broadcasted_iota(jnp.int32, (depth, depth // 2), 0) == source).astype(BF16)
    blocks = [
        jnp.dot(feats[:, k * depth : (k + 1) * depth], pick, preferred_element_type=F32).astype(BF16)
        for k in range(n_xl)
    ]
    return jnp.concatenate(blocks, axis=1)


def on_device(feats, w_qkv, grad_out, block_mask, counts):
    length = feats.shape[0]
    head = grad_out.shape[1]
    block = length // block_mask.shape[1]
    n_xl, n_z, n_dp = lax.axis_size("xl"), lax.axis_size("z"), lax.axis_size(DP)
    chips = lax.axis_size(CHIPS)
    rows, width = w_qkv.shape
    unit = rows // n_dp
    core = lax.axis_index("core")

    piece = lax.dynamic_slice_in_dim(w_qkv, lax.axis_index(DP) * unit, unit, axis=0)
    line = lax.all_to_all(jnp.broadcast_to(piece, (n_z, unit, width)), "z", 0, 0, tiled=True)
    line = line.reshape(n_z * unit, width)
    own_w = lax.all_to_all(jnp.broadcast_to(line, (chips,) + line.shape), CHIPS, 0, 0, tiled=True)
    own_w = own_w.reshape(chips * n_z * unit, width)
    other_w = lax.ppermute(own_w, "core", SWAP)

    own_feats = reordered(feats, core, n_xl, n_z, n_dp, unit)
    other_feats = reordered(feats, 1 - core, n_xl, n_z, n_dp, unit)
    qkv = jnp.dot(own_feats, own_w, preferred_element_type=F32)
    qkv = (qkv + jnp.dot(other_feats, other_w, preferred_element_type=F32)).astype(BF16)
    attended, d_qkv = attention_pass(qkv, grad_out, block_mask[0], counts[0], length, block, head)

    passed = lax.ppermute(contract_rows(other_feats, d_qkv).astype(BF16), "core", SWAP)
    chip = (contract_rows(own_feats, d_qkv) + passed.astype(F32)).astype(BF16)
    plane = lax.all_to_all(chip.reshape(chips, n_z * unit, width), CHIPS, 0, 0, tiled=True)
    plane = jnp.sum(plane.astype(F32), axis=0).astype(BF16)
    owned = lax.all_to_all(plane.reshape(n_z, unit, width), "z", 0, 0, tiled=True)
    owned = jnp.sum(owned.astype(F32), axis=0).astype(BF16)
    grad_w = lax.all_to_all(jnp.broadcast_to(owned, (n_dp, unit, width)), DP, 0, 0, tiled=True)
    return (attended, grad_w.reshape(rows, width).astype(F32))


def solution(mesh):
    fine = Mesh(mesh.devices.reshape(4, 2, 2, 2, 32), DP + SHARD)
    split = DP + SHARD
    return jax.shard_map(
        on_device,
        mesh=fine,
        in_specs=(
            P(split, None),
            P(SHARD, None),
            P(split, None),
            P(split, None, None),
            P(split),
        ),
        out_specs=(P(split, None), P(SHARD, None)),
        check_vma=False,
    )
```

```python
import jax
import jax.numpy as jnp
from jax import lax
from jax.sharding import Mesh
from jax.sharding import PartitionSpec as P

BF16 = jnp.bfloat16
F32 = jnp.float32
DP = ("y", "xh", "core")
SHARD = ("xl", "zh", "zl")
CHIPS = ("xl", "y", "xh")
REPLICAS = ("y", "xh")
SWAP = [(0, 1), (1, 0)]


def attention_pass(qkv, cotangent, mask, count, length, block, head):
    query = qkv[:, :head]
    keys = qkv[:, head : 2 * head]
    values = qkv[:, 2 * head :]
    factor = 1.0 / jnp.sqrt(F32(head))
    scores = jnp.dot(query, keys.T, preferred_element_type=F32) * factor
    expanded = jnp.repeat(jnp.repeat(mask, block, axis=0), block, axis=1)
    position = jnp.arange(length, dtype=jnp.int32)
    live = (expanded > 0) & (position[None, :] < count)
    scores = jnp.where(live, scores, F32(-1e30))
    top = jnp.max(scores, axis=1, keepdims=True)
    weight = jnp.where(live, jnp.exp(scores - top), F32(0.0))
    probs = weight / jnp.sum(weight, axis=1, keepdims=True)
    probs_b = probs.astype(BF16)
    output = jnp.dot(probs_b, values, preferred_element_type=F32).astype(BF16)
    grad_values = jnp.dot(probs_b.T, cotangent, preferred_element_type=F32)
    dprobs = jnp.dot(cotangent, values.T, preferred_element_type=F32)
    delta = jnp.sum(cotangent.astype(F32) * output.astype(F32), axis=1, keepdims=True)
    dscore = (probs * (dprobs - delta) * factor).astype(BF16)
    grad_query = jnp.dot(dscore, keys, preferred_element_type=F32)
    grad_keys = jnp.dot(dscore.T, query, preferred_element_type=F32)
    d_qkv = jnp.concatenate([grad_query, grad_keys, grad_values], axis=1).astype(BF16)
    return (output, d_qkv)


def contract_rows(columns, d_qkv):
    return lax.dot_general(columns, d_qkv, (((0,), (0,)), ((), ())), preferred_element_type=F32)


def reordered(feats, core, n_xl, n_zh, n_zl, n_dp, unit):
    depth = feats.shape[1] // n_xl
    line = n_zl * n_zh * unit
    at = lax.broadcasted_iota(jnp.int32, (depth, depth // 2), 1)
    pair, row = at // line, at % unit
    z = (at // unit) % n_zh * n_zl + (at % line) // (n_zh * unit)
    source = z * (n_dp * unit) + (2 * pair + core) * unit + row
    pick = (lax.broadcasted_iota(jnp.int32, (depth, depth // 2), 0) == source).astype(BF16)
    blocks = [
        jnp.dot(feats[:, k * depth : (k + 1) * depth], pick, preferred_element_type=F32).astype(BF16)
        for k in range(n_xl)
    ]
    return jnp.concatenate(blocks, axis=1)


def on_device(feats, w_qkv, grad_out, block_mask, counts):
    length = feats.shape[0]
    head = grad_out.shape[1]
    block = length // block_mask.shape[1]
    n_xl, n_zh, n_zl, n_dp = (lax.axis_size(axes) for axes in ("xl", "zh", "zl", DP))
    chips, replicas, cores = (lax.axis_size(axes) for axes in (CHIPS, REPLICAS, "core"))
    rows, width = w_qkv.shape
    unit = rows // n_dp
    line_rows = n_zl * n_zh * unit
    core = lax.axis_index("core")

    piece = lax.dynamic_slice_in_dim(w_qkv, lax.axis_index(DP) * unit, unit, axis=0)
    far = lax.all_to_all(jnp.broadcast_to(piece, (n_zh, unit, width)), "zh", 0, 0, tiled=True)
    far = far.reshape(n_zh * unit, width)
    line = lax.all_to_all(jnp.broadcast_to(far, (n_zl,) + far.shape), "zl", 0, 0, tiled=True)
    line = line.reshape(line_rows, width)
    own_feats = reordered(feats, core, n_xl, n_zh, n_zl, n_dp, unit)
    other_feats = reordered(feats, 1 - core, n_xl, n_zh, n_zl, n_dp, unit)
    line, own_feats, other_feats = lax.optimization_barrier((line, own_feats, other_feats))
    own_w = lax.all_to_all(jnp.broadcast_to(line, (chips,) + line.shape), CHIPS, 0, 0, tiled=True)
    own_w = own_w.reshape(chips * line_rows, width)
    other_w = lax.ppermute(own_w, "core", SWAP)

    qkv = jnp.dot(own_feats, own_w, preferred_element_type=F32)
    qkv = (qkv + jnp.dot(other_feats, other_w, preferred_element_type=F32)).astype(BF16)
    attended, d_qkv = attention_pass(qkv, grad_out, block_mask[0], counts[0], length, block, head)

    passed = lax.ppermute(contract_rows(other_feats, d_qkv).astype(BF16), "core", SWAP)
    chip = (contract_rows(own_feats, d_qkv) + passed.astype(F32)).astype(BF16)
    plane = lax.all_to_all(chip.reshape(chips, line_rows, width), CHIPS, 0, 0, tiled=True)
    plane = jnp.sum(plane.astype(F32), axis=0).astype(BF16)
    near = lax.all_to_all(plane.reshape(n_zl, n_zh * unit, width), "zl", 0, 0, tiled=True)
    near = jnp.sum(near.astype(F32), axis=0).astype(BF16).reshape(n_zh, 1, unit, width)
    near = jnp.broadcast_to(near, (n_zh, cores, unit, width)).reshape(n_zh * cores, unit, width)
    owned = lax.all_to_all(near, ("zh", "core"), 0, 0, tiled=True)
    owned = jnp.sum(owned.reshape(n_zh, cores * unit, width).astype(F32), axis=0).astype(BF16)
    grad_w = lax.all_to_all(jnp.broadcast_to(owned, (replicas,) + owned.shape), REPLICAS, 0, 0, tiled=True)
    return (attended, grad_w.reshape(rows, width).astype(F32))


def solution(mesh):
    fine = Mesh(mesh.devices.reshape(4, 2, 2, 2, 4, 8), DP + SHARD)
    split = DP + SHARD
    return jax.shard_map(
        on_device,
        mesh=fine,
        in_specs=(
            P(split, None),
            P(SHARD, None),
            P(split, None),
            P(split, None, None),
            P(split),
        ),
        out_specs=(P(split, None), P(SHARD, None)),
        check_vma=False,
    )
```

```python
import math

import jax
import jax.numpy as jnp
from jax import lax
from jax.experimental import pallas as pl
from jax.experimental.pallas import tpu as pltpu
from jax.sharding import Mesh
from jax.sharding import PartitionSpec as P

BF16 = jnp.bfloat16
F32 = jnp.float32
DP = ("y", "xh", "core")
SHARD = ("xl", "z")
PLANE = ("y", "xh", "core", "xl")
SWAP = [(0, 1), (1, 0)]
NT = (((1,), (1,)), ((), ()))
TN = (((0,), (0,)), ((), ()))


def dot(a, b, dims=(((1,), (0,)), ((), ()))):
    return lax.dot_general(a, b, dims, preferred_element_type=F32)


def attention_kernel(mask, count, mine, passed, cotangent, attended, d_qkv):
    length, head = cotangent.shape
    blocks = mask.shape[0]
    block = length // blocks
    factor = F32(1.0 / math.sqrt(head))
    qkv = (mine[...] + passed[...]).astype(BF16)
    keys, values = qkv[:, head : 2 * head], qkv[:, 2 * head :]
    position = lax.broadcasted_iota(jnp.int32, (block, length), 1)
    grad_keys = jnp.zeros((length, head), F32)
    grad_values = jnp.zeros((length, head), F32)
    for b in range(blocks):
        rows = slice(b * block, (b + 1) * block)
        query, cot = qkv[rows, :head], cotangent[rows, :]
        limit = jnp.concatenate(
            [
                jnp.full((block, block), jnp.where(mask[b, j] > 0, count[0], 0), jnp.int32)
                for j in range(blocks)
            ],
            axis=1,
        )
        live = position < limit
        scores = jnp.where(live, dot(query, keys, NT) * factor, F32(-1e30))
        top = jnp.max(scores, axis=1, keepdims=True)
        weight = jnp.where(live, jnp.exp(scores - top), F32(0.0))
        probs = weight / jnp.sum(weight, axis=1, keepdims=True)
        probs_b = probs.astype(BF16)
        out = dot(probs_b, values).astype(BF16)
        attended[rows, :] = out
        delta = jnp.sum(cot.astype(F32) * out.astype(F32), axis=1, keepdims=True)
        dscore = (probs * (dot(cot, values, NT) - delta) * factor).astype(BF16)
        d_qkv[rows, :head] = dot(dscore, keys).astype(BF16)
        grad_keys += dot(dscore, query, TN)
        grad_values += dot(probs_b, cot, TN)
    d_qkv[:, head : 2 * head] = grad_keys.astype(BF16)
    d_qkv[:, 2 * head :] = grad_values.astype(BF16)


def attention_pass(mine, passed, cotangent, mask, count):
    length, head = cotangent.shape
    vmem = pl.BlockSpec(memory_space=pltpu.VMEM)
    smem = pl.BlockSpec(memory_space=pltpu.SMEM)
    return pl.pallas_call(
        attention_kernel,
        out_shape=(
            jax.ShapeDtypeStruct((length, head), BF16),
            jax.ShapeDtypeStruct((length, 3 * head), BF16),
        ),
        in_specs=[smem, smem, vmem, vmem, vmem],
        out_specs=(vmem, vmem),
        compiler_params=pltpu.CompilerParams(vmem_limit_bytes=24 * 1024 * 1024),
        cost_estimate=pl.CostEstimate(
            flops=14 * length * length * head, bytes_accessed=2 * 1024 * 1024, transcendentals=length * length
        ),
        name="attention",
    )(mask, count, mine, passed, cotangent)


def z_at(place, n_z):
    return (place // 2 + n_z // 2 * (1 - place % 2)) % n_z


def replica_at(place):
    return (place // 4 + 2) % 4, 1 - place // 2 % 2, place % 2


def index(y, xh, core, xl):
    return ((y * 2 + xh) * 2 + core) * 2 + xl


def groups():
    places = [replica_at(p) for p in range(16)]
    chips = [[index(*places[2 * p][:2], core, xl) for xl in range(2) for p in range(8)] for core in range(2)]
    replicas = [[index(*place, xl) for place in places] for xl in range(2)]
    return [[z_at(p, 32) for p in range(32)]], chips, replicas


def reordered(feats, core, n_xl, n_z, n_dp, unit):
    depth = feats.shape[1] // n_xl
    line = n_z * unit
    at = lax.broadcasted_iota(jnp.int32, (depth, depth // 2), 1)
    pair, z, row = at // line, z_at((at % line) // unit, n_z), at % unit
    source = z * (n_dp * unit) + (2 * pair + core) * unit + row
    pick = (lax.broadcasted_iota(jnp.int32, (depth, depth // 2), 0) == source).astype(BF16)
    blocks = [dot(feats[:, k * depth : (k + 1) * depth], pick).astype(BF16) for k in range(n_xl)]
    return jnp.concatenate(blocks, axis=1)


def on_device(feats, w_qkv, grad_out, block_mask, counts):
    n_xl, n_z, n_dp = lax.axis_size("xl"), lax.axis_size("z"), lax.axis_size(DP)
    chips = 16
    rows, width = w_qkv.shape
    unit = rows // n_dp
    core = lax.axis_index("core")

    theirs = lax.ppermute(reordered(feats, 1 - core, n_xl, n_z, n_dp, unit), "core", SWAP)
    own_feats = reordered(feats, core, n_xl, n_z, n_dp, unit)

    lines, plane_chips, replicas = groups()
    place = (lax.axis_index("y") + 2) % 4 * 4 + (1 - lax.axis_index("xh")) * 2 + core
    piece = lax.dynamic_slice_in_dim(w_qkv, place * unit, unit, axis=0)
    line = lax.all_to_all(jnp.broadcast_to(piece, (n_z, unit, width)), "z", 0, 0, axis_index_groups=lines, tiled=True)
    line = line.reshape(n_z * unit, width)
    line, theirs, own_feats = lax.optimization_barrier((line, theirs, own_feats))
    own_w = lax.all_to_all(jnp.broadcast_to(line, (chips,) + line.shape), PLANE, 0, 0, axis_index_groups=plane_chips, tiled=True)
    own_w = own_w.reshape(chips * n_z * unit, width)

    passed = lax.ppermute(dot(theirs, own_w), "core", SWAP)
    attended, d_qkv = attention_pass(dot(own_feats, own_w), passed, grad_out, block_mask[0], counts)

    d_theirs = lax.ppermute(d_qkv, "core", SWAP)
    own_part = lax.optimization_barrier(dot(own_feats, d_qkv, TN))
    chip = (own_part + dot(theirs, d_theirs, TN)).astype(BF16)
    plane = lax.all_to_all(chip.reshape(chips, n_z * unit, width), PLANE, 0, 0, axis_index_groups=plane_chips, tiled=True)
    plane = jnp.sum(plane.astype(F32), axis=0).astype(BF16)
    owned = lax.all_to_all(plane.reshape(n_z, unit, width), "z", 0, 0, axis_index_groups=lines, tiled=True)
    owned = jnp.sum(owned.astype(F32), axis=0).astype(BF16)
    grad_w = lax.all_to_all(jnp.broadcast_to(owned, (n_dp, unit, width)), PLANE, 0, 0, axis_index_groups=replicas, tiled=True)
    return (attended, grad_w.reshape(rows, width).astype(F32))


def solution(mesh):
    fine = Mesh(mesh.devices.reshape(4, 2, 2, 2, 32), DP + SHARD)
    split = DP + SHARD
    return jax.shard_map(
        on_device,
        mesh=fine,
        in_specs=(
            P(split, None),
            P(SHARD, None),
            P(split, None),
            P(split, None, None),
            P(split),
        ),
        out_specs=(P(split, None), P(SHARD, None)),
        check_vma=False,
    )
```

```python
import math

import jax
import jax.numpy as jnp
from jax import lax
from jax.experimental import pallas as pl
from jax.experimental.pallas import tpu as pltpu
from jax.sharding import Mesh
from jax.sharding import PartitionSpec as P

BF16 = jnp.bfloat16
F32 = jnp.float32
DP = ("y", "xh", "core")
SHARD = ("xl", "z")
PLANE = ("y", "xh", "core", "xl")
SWAP = [(0, 1), (1, 0)]
NT = (((1,), (1,)), ((), ()))
TN = (((0,), (0,)), ((), ()))


def dot(a, b, dims=(((1,), (0,)), ((), ()))):
    return lax.dot_general(a, b, dims, preferred_element_type=F32)


def attention_kernel(mask, count, mine, passed, cotangent, attended, d_qkv):
    length, head = cotangent.shape
    blocks = mask.shape[0]
    block = length // blocks
    factor = F32(1.0 / math.sqrt(head))
    qkv = (mine[...] + passed[...]).astype(BF16)
    query, keys, values = qkv[:, :head], qkv[:, head : 2 * head], qkv[:, 2 * head :]
    limit = jnp.concatenate(
        [
            jnp.concatenate(
                [
                    jnp.full((block, block), jnp.where(mask[i, j] > 0, count[0], 0), jnp.int32)
                    for j in range(blocks)
                ],
                axis=1,
            )
            for i in range(blocks)
        ],
        axis=0,
    )
    live = lax.broadcasted_iota(jnp.int32, (length, length), 1) < limit
    scores = jnp.where(live, dot(query, keys, NT) * factor, F32(-1e30))
    top = jnp.max(scores, axis=1, keepdims=True)
    weight = jnp.where(live, jnp.exp(scores - top), F32(0.0))
    probs = weight / jnp.sum(weight, axis=1, keepdims=True)
    probs_b = probs.astype(BF16)
    out = dot(probs_b, values).astype(BF16)
    attended[...] = out
    cot = cotangent[...]
    delta = jnp.sum(cot.astype(F32) * out.astype(F32), axis=1, keepdims=True)
    dscore = (probs * (dot(cot, values, NT) - delta) * factor).astype(BF16)
    d_qkv[:, :head] = dot(dscore, keys).astype(BF16)
    d_qkv[:, head : 2 * head] = dot(query, dscore, TN).T.astype(BF16)
    d_qkv[:, 2 * head :] = dot(cot, probs_b, TN).T.astype(BF16)


def attention_pass(mine, passed, cotangent, mask, count):
    length, head = cotangent.shape
    vmem = pl.BlockSpec(memory_space=pltpu.VMEM)
    smem = pl.BlockSpec(memory_space=pltpu.SMEM)
    return pl.pallas_call(
        attention_kernel,
        out_shape=(
            jax.ShapeDtypeStruct((length, head), BF16),
            jax.ShapeDtypeStruct((length, 3 * head), BF16),
        ),
        in_specs=[smem, smem, vmem, vmem, vmem],
        out_specs=(vmem, vmem),
        compiler_params=pltpu.CompilerParams(vmem_limit_bytes=24 * 1024 * 1024),
        cost_estimate=pl.CostEstimate(
            flops=14 * length * length * head, bytes_accessed=2 * 1024 * 1024, transcendentals=length * length
        ),
        name="attention",
    )(mask, count, mine, passed, cotangent)


def z_at(place, n_z):
    return (place // 2 + n_z // 2 * (1 - place % 2)) % n_z


def replica_at(place):
    return (place // 4 + 2) % 4, 1 - place // 2 % 2, place % 2


def index(y, xh, core, xl):
    return ((y * 2 + xh) * 2 + core) * 2 + xl


def groups():
    places = [replica_at(p) for p in range(16)]
    chips = [[index(*places[2 * p][:2], core, xl) for xl in range(2) for p in range(8)] for core in range(2)]
    replicas = [[index(*place, xl) for place in places] for xl in range(2)]
    return [[z_at(p, 32) for p in range(32)]], chips, replicas


def reordered(feats, core, n_xl, n_z, n_dp, unit):
    depth = feats.shape[1] // n_xl
    line = n_z * unit
    at = lax.broadcasted_iota(jnp.int32, (depth, depth // 2), 1)
    pair, z, row = at // line, z_at((at % line) // unit, n_z), at % unit
    source = z * (n_dp * unit) + (2 * pair + core) * unit + row
    pick = (lax.broadcasted_iota(jnp.int32, (depth, depth // 2), 0) == source).astype(BF16)
    blocks = [dot(feats[:, k * depth : (k + 1) * depth], pick).astype(BF16) for k in range(n_xl)]
    return jnp.concatenate(blocks, axis=1)


def on_device(feats, w_qkv, grad_out, block_mask, counts):
    n_xl, n_z, n_dp = lax.axis_size("xl"), lax.axis_size("z"), lax.axis_size(DP)
    chips = 16
    rows, width = w_qkv.shape
    unit = rows // n_dp
    core = lax.axis_index("core")

    theirs = lax.ppermute(reordered(feats, 1 - core, n_xl, n_z, n_dp, unit), "core", SWAP)
    own_feats = reordered(feats, core, n_xl, n_z, n_dp, unit)

    lines, plane_chips, replicas = groups()
    place = (lax.axis_index("y") + 2) % 4 * 4 + (1 - lax.axis_index("xh")) * 2 + core
    piece = lax.dynamic_slice_in_dim(w_qkv, place * unit, unit, axis=0)
    line = lax.all_to_all(jnp.broadcast_to(piece, (n_z, unit, width)), "z", 0, 0, axis_index_groups=lines, tiled=True)
    line = line.reshape(n_z * unit, width)
    line, theirs, own_feats = lax.optimization_barrier((line, theirs, own_feats))
    own_w = lax.all_to_all(jnp.broadcast_to(line, (chips,) + line.shape), PLANE, 0, 0, axis_index_groups=plane_chips, tiled=True)
    own_w = own_w.reshape(chips * n_z * unit, width)

    passed = lax.ppermute(dot(theirs, own_w), "core", SWAP)
    attended, d_qkv = attention_pass(dot(own_feats, own_w), passed, grad_out, block_mask[0], counts)

    d_theirs = lax.ppermute(d_qkv, "core", SWAP)
    own_part = lax.optimization_barrier(dot(own_feats, d_qkv, TN))
    chip = (own_part + dot(theirs, d_theirs, TN)).astype(BF16)
    plane = lax.all_to_all(chip.reshape(chips, n_z * unit, width), PLANE, 0, 0, axis_index_groups=plane_chips, tiled=True)
    plane = jnp.sum(plane.astype(F32), axis=0).astype(BF16)
    owned = lax.all_to_all(plane.reshape(n_z, unit, width), "z", 0, 0, axis_index_groups=lines, tiled=True)
    owned = jnp.sum(owned.astype(F32), axis=0).astype(BF16)
    grad_w = lax.all_to_all(jnp.broadcast_to(owned, (n_dp, unit, width)), PLANE, 0, 0, axis_index_groups=replicas, tiled=True)
    return (attended, grad_w.reshape(rows, width).astype(F32))


def solution(mesh):
    fine = Mesh(mesh.devices.reshape(4, 2, 2, 2, 32), DP + SHARD)
    split = DP + SHARD
    return jax.shard_map(
        on_device,
        mesh=fine,
        in_specs=(
            P(split, None),
            P(SHARD, None),
            P(split, None),
            P(split, None, None),
            P(split),
        ),
        out_specs=(P(split, None), P(SHARD, None)),
        check_vma=False,
    )
```

```python
import math

import jax
import jax.numpy as jnp
from jax import lax
from jax.experimental import pallas as pl
from jax.experimental.pallas import tpu as pltpu
from jax.sharding import Mesh
from jax.sharding import PartitionSpec as P

BF16 = jnp.bfloat16
F32 = jnp.float32
DP = ("y", "xh", "core")
SHARD = ("xl", "z")
PLANE = ("y", "xh", "core", "xl")
AHEAD = 4
SWAP = [(0, 1), (1, 0)]
NT = (((1,), (1,)), ((), ()))
TN = (((0,), (0,)), ((), ()))


def dot(a, b, dims=(((1,), (0,)), ((), ()))):
    return lax.dot_general(a, b, dims, preferred_element_type=F32)


def attention_kernel(mask, count, mine, passed, cotangent, attended, d_qkv):
    length, head = cotangent.shape
    blocks = mask.shape[0]
    block = length // blocks
    factor = F32(1.0 / math.sqrt(head))
    qkv = (mine[...] + passed[...]).astype(BF16)
    query, keys, values = qkv[:, :head], qkv[:, head : 2 * head], qkv[:, 2 * head :]
    limit = jnp.concatenate(
        [
            jnp.concatenate(
                [
                    jnp.full((block, block), jnp.where(mask[i, j] > 0, count[0], 0), jnp.int32)
                    for j in range(blocks)
                ],
                axis=1,
            )
            for i in range(blocks)
        ],
        axis=0,
    )
    live = lax.broadcasted_iota(jnp.int32, (length, length), 1) < limit
    scores = jnp.where(live, dot(query, keys, NT) * factor, F32(-1e30))
    top = jnp.max(scores, axis=1, keepdims=True)
    weight = jnp.where(live, jnp.exp(scores - top), F32(0.0))
    probs = weight / jnp.sum(weight, axis=1, keepdims=True)
    probs_b = probs.astype(BF16)
    out = dot(probs_b, values).astype(BF16)
    attended[...] = out
    cot = cotangent[...]
    delta = jnp.sum(cot.astype(F32) * out.astype(F32), axis=1, keepdims=True)
    dscore = (probs * (dot(cot, values, NT) - delta) * factor).astype(BF16)
    d_qkv[:, :head] = dot(dscore, keys).astype(BF16)
    d_qkv[:, head : 2 * head] = dot(query, dscore, TN).T.astype(BF16)
    d_qkv[:, 2 * head :] = dot(cot, probs_b, TN).T.astype(BF16)


def attention_pass(mine, passed, cotangent, mask, count):
    length, head = cotangent.shape
    vmem = pl.BlockSpec(memory_space=pltpu.VMEM)
    smem = pl.BlockSpec(memory_space=pltpu.SMEM)
    return pl.pallas_call(
        attention_kernel,
        out_shape=(
            jax.ShapeDtypeStruct((length, head), BF16),
            jax.ShapeDtypeStruct((length, 3 * head), BF16),
        ),
        in_specs=[smem, smem, vmem, vmem, vmem],
        out_specs=(vmem, vmem),
        compiler_params=pltpu.CompilerParams(vmem_limit_bytes=24 * 1024 * 1024),
        cost_estimate=pl.CostEstimate(
            flops=14 * length * length * head, bytes_accessed=2 * 1024 * 1024, transcendentals=length * length
        ),
        name="attention",
    )(mask, count, mine, passed, cotangent)


def z_at(place, n_z):
    return (place + n_z // 2) % n_z


def replica_at(place):
    return (place // 4 + 2) % 4, 1 - place // 2 % 2, place % 2


def index(y, xh, core, xl):
    return ((y * 2 + xh) * 2 + core) * 2 + xl


def groups():
    places = [replica_at(p) for p in range(16)]
    chips = [[index(*places[2 * p][:2], core, xl) for xl in range(2) for p in range(8)] for core in range(2)]
    replicas = [[index(*place, xl) for place in places] for xl in range(2)]
    return [[z_at(p + AHEAD, 32) for p in range(32)]], [[z_at(p, 32) for p in range(32)]], chips, replicas


def reordered(feats, core, n_xl, n_z, n_dp, unit):
    depth = feats.shape[1] // n_xl
    line = n_z * unit
    at = lax.broadcasted_iota(jnp.int32, (depth, depth // 2), 1)
    pair, z, row = at // line, z_at((at % line) // unit, n_z), at % unit
    source = z * (n_dp * unit) + (2 * pair + core) * unit + row
    pick = (lax.broadcasted_iota(jnp.int32, (depth, depth // 2), 0) == source).astype(BF16)
    blocks = [dot(feats[:, k * depth : (k + 1) * depth], pick).astype(BF16) for k in range(n_xl)]
    return jnp.concatenate(blocks, axis=1)


def on_device(feats, w_qkv, grad_out, block_mask, counts):
    n_xl, n_z, n_dp = lax.axis_size("xl"), lax.axis_size("z"), lax.axis_size(DP)
    chips = 16
    rows, width = w_qkv.shape
    unit = rows // n_dp
    core = lax.axis_index("core")

    theirs = lax.ppermute(reordered(feats, 1 - core, n_xl, n_z, n_dp, unit), "core", SWAP)
    own_feats = reordered(feats, core, n_xl, n_z, n_dp, unit)

    lines_in, lines_back, plane_chips, replicas = groups()
    place = (lax.axis_index("y") + 2) % 4 * 4 + (1 - lax.axis_index("xh")) * 2 + core
    piece = lax.dynamic_slice_in_dim(w_qkv, place * unit, unit, axis=0)
    line = lax.all_to_all(jnp.broadcast_to(piece, (n_z, unit, width)), "z", 0, 0, axis_index_groups=lines_in, tiled=True)
    line = jnp.roll(line, AHEAD, axis=0).reshape(n_z * unit, width)
    line, theirs, own_feats = lax.optimization_barrier((line, theirs, own_feats))
    own_w = lax.all_to_all(jnp.broadcast_to(line, (chips,) + line.shape), PLANE, 0, 0, axis_index_groups=plane_chips, tiled=True)
    own_w = own_w.reshape(chips * n_z * unit, width)

    passed = lax.ppermute(dot(theirs, own_w), "core", SWAP)
    attended, d_qkv = attention_pass(dot(own_feats, own_w), passed, grad_out, block_mask[0], counts)

    d_theirs = lax.ppermute(d_qkv, "core", SWAP)
    own_part = lax.optimization_barrier(dot(own_feats, d_qkv, TN))
    chip = (own_part + dot(theirs, d_theirs, TN)).astype(BF16)
    plane = lax.all_to_all(chip.reshape(chips, n_z * unit, width), PLANE, 0, 0, axis_index_groups=plane_chips, tiled=True)
    plane = jnp.sum(plane.astype(F32), axis=0).astype(BF16)
    owned = lax.all_to_all(plane.reshape(n_z, unit, width), "z", 0, 0, axis_index_groups=lines_back, tiled=True)
    owned = jnp.sum(owned.astype(F32), axis=0).astype(BF16)
    grad_w = lax.all_to_all(jnp.broadcast_to(owned, (n_dp, unit, width)), PLANE, 0, 0, axis_index_groups=replicas, tiled=True)
    return (attended, grad_w.reshape(rows, width).astype(F32))


def solution(mesh):
    fine = Mesh(mesh.devices.reshape(4, 2, 2, 2, 32), DP + SHARD)
    split = DP + SHARD
    return jax.shard_map(
        on_device,
        mesh=fine,
        in_specs=(
            P(split, None),
            P(SHARD, None),
            P(split, None),
            P(split, None, None),
            P(split),
        ),
        out_specs=(P(split, None), P(SHARD, None)),
        check_vma=False,
    )
```
